32 devices in a mesh: grp: 4 (over z), ord: 8 (over y, x, core).
Axes of the slice: x: 2, y: 2, z: 4, core: 2. Of those that a mesh axis runs over, the one named last changes fastest.
Arguments:
- legendre: float32 [512, 131072], P('ord', 'grp')
- lon_center: float32 [4], P('grp'), may hold values from 0 to 1
- counts: int32 [4, 8], P('grp'), may hold values from 1 to 4096, 24576 in all within a row
- column_index: int32 [3, 512], replicated, may hold values from 0 to 120, as said below
Outputs:
- factor: float32 [512, 512], replicated
The draws below stay inside these ranges and needn't reach their ends.
Inputs may be any that keep to these rules, and one draw needn't show every extreme that they name: `column_index`: each column names a different coefficient: row 0 is its degree (at most 120), row 1 its order (at most the degree), row 2 is 1 for a sine term and 0 for a cosine term, and 0 at order 0. Each group's counts add up to 24576.
All inputs are finite; a program needn't handle non-finite values.
Results may differ from the reference program's by a relative error of at most 0.0003.
Values sent between devices are 32-bit elements; how exact they have to be, the bound alone decides.
No kernel may reach another device: no remote copies, remote signals or barrier semaphores. Data moves between devices by JAX's collectives and lax.ppermute only.
A program may use at most 64 MiB of HBM per device.

```python
import math
import jax
import jax.numpy as jnp
import numpy as np
from jax import lax

NMAX = 120
COLS = 512
ROWS_DEV = 4096
ROWS_GRP = 32768
ROWS = 131072
N_GRP = 4
N_ORD = 8


def draw_legendre(key, part):
    key_rough, key_common, key_column, key_shared = jax.random.split(key, 4)
    rough_part = jax.random.normal(key_rough, (COLS, ROWS), jnp.float32)
    common_row = jax.random.normal(key_common, (ROWS,), jnp.float32)
    column_gain = jnp.exp(jax.random.uniform(key_column, (COLS,), jnp.float32, -0.693, 0.693))
    common_gain = jax.random.uniform(key_shared, (COLS,), jnp.float32, 0.4, 1.2)
    position = jnp.arange(ROWS, dtype=jnp.float32) / (ROWS - 1)
    row_scale = 0.5 + position
    mixed = rough_part + common_gain[:, None] * common_row[None, :]
    return column_gain[:, None] * row_scale[None, :] * mixed


def draw_column_index(key, part):
    entries = []
    for degree in range(NMAX + 1):
        for harmonic_order in range(degree + 1):
            flags = (0,) if harmonic_order == 0 else (0, 1)
            for sine_flag in flags:
                entries.append((degree, harmonic_order, sine_flag))
    lookup = jnp.asarray(np.array(entries, dtype=np.int32).T)
    chosen = jax.random.permutation(key, lookup.shape[1])[:COLS]
    return lookup[:, chosen].astype(jnp.int32)


def levels(own_key, extent, shards, least, high):
    factor_of = 1.0
    for dim, parts in shards:
        steps = jax.random.uniform(jax.random.fold_in(jax.random.fold_in(own_key, 6), dim), (parts,), jnp.float32, least / len(shards), high / len(shards))
        factor_of = factor_of * jnp.repeat(jnp.exp(steps), extent[dim] // parts).reshape((-1,) + (1,) * (len(extent) - 1 - dim))
    return factor_of


def length_profile(amount, total, limit, skew):
    loads = [(1 << 20) // math.isqrt(rank ** skew) + 1 for rank in range(2, amount + 1)]
    spare, given = total - limit - (amount - 1), [1] * (amount - 1)
    while spare > 0:
        free = [i for i in range(amount - 1) if given[i] < limit]
        pool, left = sum([loads[i] for i in free]), spare
        for i in free:
            addition = min(limit - given[i], max(1, left * loads[i] // pool), spare)
            given[i] = given[i] + addition
            spare = spare - addition
    return np.array([limit] + given)


def ragged_sizes(own_key, number_of, total, bound, slope):
    if number_of == 2:
        one = jax.random.randint(own_key, (), max(1, total - bound), min(bound, total - 1) + 1)
        return jnp.stack([one, total - one])
    tallies = jnp.asarray(length_profile(number_of, total, bound, slope), jnp.int32)
    couples = (number_of - 1) // 2
    donor, sink = tallies[1:1 + 2 * couples:2], tallies[2:2 + 2 * couples:2]
    slack = jnp.minimum(donor - 1, bound - sink)
    moved = jax.random.randint(jax.random.fold_in(own_key, 1), (couples,), 0, 1 << 20) % (slack + 1)
    tallies = tallies.at[1:1 + 2 * couples:2].set(donor - moved).at[2:2 + 2 * couples:2].set(sink + moved)
    return tallies[jax.random.permutation(jax.random.fold_in(own_key, 2), number_of)]


def setup_inputs(seed: int = 0) -> dict:
    key_of = jax.random.split(jax.random.key(seed), 5)
    return {
        "legendre": draw_legendre(jax.random.fold_in(key_of[4], 71), 0),
        "lon_center": jnp.clip(1.0 * jax.random.uniform(key_of[1], (N_GRP,), jnp.float32) ** levels(key_of[1], (N_GRP,), ((0, 4),), -0.2, 0.2), 0.0, 1.0),
        "counts": jax.vmap(lambda own: ragged_sizes(own, N_ORD, N_ORD * ROWS_DEV * 3 // 4, ROWS_DEV, 2))(jax.random.split(key_of[2], N_GRP)).reshape((N_GRP, N_ORD)).astype(jnp.int32),
        "column_index": draw_column_index(jax.random.fold_in(key_of[4], 71), 0),
    }


quarter_turn = math.pi / 2
track_span = 0.3
kaula_gain = 1.2

def reference(legendre, lon_center, counts, column_index):
    harmonic = column_index[1].astype(jnp.float32)
    sine_part = column_index[2].astype(jnp.float32)
    along = jnp.arange(ROWS_GRP, dtype=jnp.float32) * (track_span / ROWS_GRP)
    slot_index = jnp.arange(ROWS_DEV, dtype=jnp.int32)
    scaling = 1.0 / math.sqrt(ROWS)

    def one_group(total, group):
        start = (group * ROWS_GRP).astype(jnp.int32)
        rows_block = lax.dynamic_slice_in_dim(legendre, start, ROWS_GRP, 1)
        longitude = lon_center[group] + along
        harmonic_wave = jnp.cos(harmonic[:, None] * longitude[None, :] - sine_part[:, None] * quarter_turn)
        row_valid = (slot_index[None, :] < counts[group][:, None]).astype(jnp.float32).reshape(ROWS_GRP)
        design = rows_block * harmonic_wave * (row_valid * scaling)[None, :]
        return (total + jnp.dot(design, design.T, precision=lax.Precision.HIGHEST), None)
    gram, _ = lax.scan(one_group, jnp.zeros((COLS, COLS), jnp.float32), jnp.arange(N_GRP, dtype=jnp.int32))
    degree = column_index[0].astype(jnp.float32)
    kaula_weight = kaula_gain * (degree / NMAX) ** 2
    normal = gram + jnp.diag(kaula_weight * kaula_weight)
    return jnp.linalg.cholesky(normal).T
```

```python
import functools
import math

import jax
import jax.numpy as jnp
from jax import lax
from jax.experimental import pallas as pl
from jax.experimental.pallas import tpu as pltpu
from jax.sharding import PartitionSpec as P

NMAX = 120
LANES = 128
SUBS = 8

quarter_turn = math.pi / 2
track_span = 0.3
kaula_gain = 1.2
VMEM = pltpu.VMEM
SMEM = pltpu.SMEM


def cosine(x):
    turns = jnp.floor(x * (1.0 / math.pi) + 0.5)
    rest = x - turns * 3.140625
    rest = rest - turns * 9.670257568359375e-4
    rest = rest - turns * 6.2770535e-7
    half = turns * 0.5
    sign = 1.0 - 4.0 * (half - jnp.floor(half))
    sq = rest * rest
    acc = jnp.full_like(x, 1.0 / math.factorial(14))
    acc = -1.0 * acc
    for power, s in ((12, 1.0), (10, -1.0), (8, 1.0), (6, -1.0), (4, 1.0), (2, -1.0), (0, 1.0)):
        acc = acc * sq + s / math.factorial(power)
    return acc * sign


def loop(count, step):
    lax.fori_loop(0, count, step, 0, unroll=5 if count % 5 == 0 else 1)


def design_kernel(shape, k, counts_ref, lon_ref, index_ref, leg_ref, *refs):
    n, sizes, rows_dev, rows_grp, scaling = shape
    outs, (held, table, sems) = refs[: len(sizes)], refs[len(sizes) :]
    blocks_dev, per = rows_dev // LANES, sum(sizes)
    me = lax.axis_index("ord")
    dest = me ^ k
    ends, total = [], 0
    for r in range(n):
        total = total + lax.div(counts_ref[0, r] + (LANES - 1), LANES)
        ends.append(total)

    def copy(i, start):
        return pltpu.make_async_copy(
            leg_ref.at[:, pl.ds(pl.multiple_of(start, LANES), LANES)],
            held.at[:, pl.ds(pl.multiple_of(i * LANES, LANES), LANES)],
            sems.at[i],
        )

    def plan(i, _):
        want = dest * per + i
        slot, first, count = 0, 0, counts_ref[0, 0]
        for r in range(n - 1):
            past = want >= ends[r]
            slot = jnp.where(past, r + 1, slot)
            first = jnp.where(past, ends[r], first)
            count = jnp.where(past, counts_ref[0, r + 1], count)
        inside = jnp.minimum(want - first, blocks_dev - 1)
        start = slot * rows_dev + inside * LANES
        copy(i, start).start()
        table[0, i] = start
        table[1, i] = jnp.where(want < total, count - (want - first) * LANES, 0)
        return 0

    loop(per, plan)
    rows = held.shape[0]
    wide = (rows, index_ref.shape[1])
    mine = lax.broadcasted_iota(jnp.int32, wide, 1) == lax.broadcasted_iota(jnp.int32, wide, 0) + me * rows

    def column(row):
        values = jnp.broadcast_to(index_ref[row : row + 1, :].astype(jnp.float32), wide)
        picked = jnp.sum(jnp.where(mine, values, 0.0), axis=1, keepdims=True)
        return jnp.broadcast_to(picked, (rows, LANES))

    harmonic = column(1)
    phase = column(2) * quarter_turn
    lane = lax.broadcasted_iota(jnp.int32, (SUBS, LANES), 1)
    base = 0
    for out_ref, size in zip(outs, sizes):

        def work(i, _, out_ref=out_ref, base=base):
            copy(base + i, 0).wait()
            along = (table[0, base + i] + lane).astype(jnp.float32) * (track_span / rows_grp)
            longitude = lon_ref[0] + along
            gate = jnp.where(lane < table[1, base + i], scaling, 0.0)
            there = pl.ds(pl.multiple_of((base + i) * LANES, LANES), LANES)
            here = pl.ds(pl.multiple_of(i * LANES, LANES), LANES)
            for top in range(0, rows, SUBS):
                wave = cosine(harmonic[top : top + SUBS] * longitude - phase[top : top + SUBS])
                out_ref[pl.ds(top, SUBS), here] = held[pl.ds(top, SUBS), there] * wave * gate
            return 0

        loop(size, work)
        base += size


@functools.partial(jax.jit, static_argnums=(0, 1))
def design_for(shape, k, counts, lon_center, column_index, legendre):
    n, sizes, rows_dev, rows_grp, _ = shape
    rows, per = legendre.shape[0], sum(sizes)
    elements = rows * per * LANES
    return pl.pallas_call(
        functools.partial(design_kernel, shape, k),
        out_shape=[jax.ShapeDtypeStruct((rows, size * LANES), jnp.float32) for size in sizes],
        in_specs=[
            pl.BlockSpec(memory_space=SMEM),
            pl.BlockSpec(memory_space=SMEM),
            pl.BlockSpec(memory_space=VMEM),
            pl.BlockSpec(memory_space=pltpu.HBM),
        ],
        out_specs=[pl.BlockSpec(memory_space=VMEM)] * len(sizes),
        scratch_shapes=[
            pltpu.VMEM((rows, per * LANES), jnp.float32),
            pltpu.SMEM((2, per), jnp.int32),
            pltpu.SemaphoreType.DMA((per,)),
        ],
        compiler_params=pltpu.CompilerParams(vmem_limit_bytes=16 << 20),
        cost_estimate=pl.CostEstimate(flops=30 * elements, bytes_accessed=8 * elements, transcendentals=0),
        name="design",
    )(counts, lon_center, column_index, legendre)


def upper_blocks(cols):
    nb = cols // LANES
    return [(i, j) for i in range(nb) for j in range(i, nb)]


def gram_kernel(n, cols, first, last, *refs):
    ins, refs = refs[:n], refs[n:]
    before = None
    if not first:
        before, refs = refs[0], refs[1:]
    outs, scratch = refs[: n if last else 1], refs[n if last else 1 :]
    high, low = scratch[:2]
    acc = scratch[2] if last else outs[0]
    me = lax.axis_index("ord")
    each = cols // n
    for k in range(n):
        tile = ins[k][...]
        at = pl.ds(pl.multiple_of((me ^ k) * each, each), each)
        top = tile.astype(jnp.bfloat16)
        high[at, :] = top
        low[at, :] = (tile - top.astype(jnp.float32)).astype(jnp.bfloat16)

    def times(a, b):
        return lax.dot_general(a, b, (((1,), (1,)), ((), ())), preferred_element_type=jnp.float32)

    step = pl.program_id(0)
    tall = min(256, cols)
    for i in range(0, cols, tall):
        hi, lo = high[pl.ds(i, tall), :], low[pl.ds(i, tall), :]
        his, los = high[pl.ds(i, cols - i), :], low[pl.ds(i, cols - i), :]
        at = (pl.ds(i, tall), pl.ds(i, cols - i))
        here = times(hi, his) + (times(hi, los) + times(lo, his))

        @pl.when(step == 0)
        def _():
            acc[at] = here if first else before[at] + here

        @pl.when(step > 0)
        def _():
            acc[at] += here

    if last:
        packed = scratch[3]

        @pl.when(step == pl.num_programs(0) - 1)
        def _():
            for t, (i, j) in enumerate(upper_blocks(cols)):
                packed[pl.ds(t * LANES, LANES), :] = acc[pl.ds(i * LANES, LANES), pl.ds(j * LANES, LANES)]
            piece = packed.shape[0] // n
            for k in range(n):
                outs[k][...] = packed[pl.ds(pl.multiple_of((me ^ k) * piece, SUBS), piece), :]


def gram(n, parts, before, last):
    each, rows = parts[0].shape
    cols = each * n
    tile = 640 if rows % 640 == 0 else LANES
    height = len(upper_blocks(cols)) * LANES
    whole = pl.BlockSpec((cols, cols), lambda s: (0, 0))
    in_specs = [pl.BlockSpec((each, tile), lambda s: (0, s))] * n + [whole] * len(before)
    scratch = [pltpu.VMEM((cols, tile), jnp.bfloat16)] * 2
    if last:
        out_shape = [jax.ShapeDtypeStruct((height // n, LANES), jnp.float32)] * n
        out_specs = [pl.BlockSpec((height // n, LANES), lambda s: (0, 0))] * n
        scratch += [pltpu.VMEM((cols, cols), jnp.float32), pltpu.VMEM((height, LANES), jnp.float32)]
    else:
        out_shape, out_specs = [jax.ShapeDtypeStruct((cols, cols), jnp.float32)], [whole]
    return pl.pallas_call(
        functools.partial(gram_kernel, n, cols, not before, last),
        grid=(rows // tile,),
        out_shape=out_shape,
        in_specs=in_specs,
        out_specs=out_specs,
        scratch_shapes=scratch,
        compiler_params=pltpu.CompilerParams(vmem_limit_bytes=32 << 20),
        cost_estimate=pl.CostEstimate(
            flops=6 * cols * cols * rows, bytes_accessed=4 * cols * rows, transcendentals=0
        ),
        name="gram",
    )(*parts, *before)


def lane_wide(x, j):
    return jnp.broadcast_to(x[:, j : j + 1], (SUBS, LANES))


def sub_wide(x, i):
    return jnp.broadcast_to(x[i : i + 1, :], (SUBS, LANES))


def factor_panel(a_ref, r_ref, base, p, wide, lane, sub):
    groups = LANES // SUBS
    row0, c0 = base + SUBS * p, SUBS * p
    own = [a_ref[pl.ds(row0, SUBS), pl.ds(base + LANES * w, LANES)] for w in range(wide)]
    spread = [lane_wide(own[0], c0 + j) for j in range(SUBS)]
    d = {(i, j): sub_wide(spread[j], i) for j in range(SUBS) for i in range(j + 1)}
    inv, up = [None] * SUBS, {}
    for i in range(SUBS):
        inv[i] = lax.rsqrt(d[i, i])
        for j in range(i + 1, SUBS):
            up[i, j] = d[i, j] * inv[i]
        for a in range(i + 1, SUBS):
            for b in range(a, SUBS):
                d[a, b] = d[a, b] - up[i, a] * up[i, b]
    done = [[None] * SUBS for _ in range(wide)]
    for w in range(wide):
        for i in range(SUBS):
            acc = sub_wide(own[w], i)
            for j in range(i):
                acc = acc - up[j, i] * done[w][j]
            done[w][i] = acc * inv[i]
        out = done[w][0]
        for i in range(1, SUBS):
            out = jnp.where(sub == i, done[w][i], out)
        if w == 0:
            out = jnp.where(lane >= sub + c0, out, 0.0)
        r_ref[pl.ds(row0, SUBS), pl.ds(base + LANES * w, LANES)] = out

    def update(g, coef, rows):
        for w in range(wide):
            at = (pl.ds(base + SUBS * g, SUBS), pl.ds(base + LANES * w, LANES))
            total = coef[0] * rows[w][0]
            for j in range(1, SUBS):
                total = total + coef[j] * rows[w][j]
            a_ref[at] = a_ref[at] - total

    if p + 1 < groups:
        below = a_ref[pl.ds(base + SUBS * (p + 1), SUBS), pl.ds(base, LANES)]
        coef = []
        for j in range(SUBS):
            acc = lane_wide(below, c0 + j)
            for i in range(j):
                acc = acc - up[i, j] * coef[i]
            coef.append(acc * inv[j])
        update(p + 1, coef, done)
    if p + 2 < groups:
        solved = [[None] * SUBS for _ in range(wide)]
        for w in range(wide):
            for i in range(SUBS - 1, -1, -1):
                acc = done[w][i]
                for j in range(i + 1, SUBS):
                    acc = acc - up[i, j] * solved[w][j]
                solved[w][i] = acc * inv[i]
        for g in range(p + 2, groups):
            below = a_ref[pl.ds(base + SUBS * g, SUBS), pl.ds(base, LANES)]
            update(g, [lane_wide(below, c0 + j) for j in range(SUBS)], solved)


def factor_kernel(n, cols, kaula_ref, *refs):
    ins, r_ref, a_ref, packed = refs[:n], refs[n], refs[n + 1], refs[n + 2]
    me = lax.axis_index("ord")
    piece = packed.shape[0] // n
    for k in range(n):
        packed[pl.ds(pl.multiple_of((me ^ k) * piece, SUBS), piece), :] = ins[k][...]
    square = (LANES, LANES)
    diag = lax.broadcasted_iota(jnp.int32, square, 0) == lax.broadcasted_iota(jnp.int32, square, 1)
    for t, (i, j) in enumerate(upper_blocks(cols)):
        block = packed[pl.ds(t * LANES, LANES), :]
        if i == j:
            block = block + jnp.where(diag, kaula_ref[:, pl.ds(i * LANES, LANES)], 0.0)
        a_ref[pl.ds(i * LANES, LANES), pl.ds(j * LANES, LANES)] = block
    lane = lax.broadcasted_iota(jnp.int32, (SUBS, LANES), 1)
    sub = lax.broadcasted_iota(jnp.int32, (SUBS, LANES), 0)
    count = cols // LANES
    for k in range(count):
        base, wide = k * LANES, count - k
        if base:
            r_ref[pl.ds(base, LANES), pl.ds(0, base)] = jnp.zeros((LANES, base), jnp.float32)
        for p in range(LANES // SUBS):
            factor_panel(a_ref, r_ref, base, p, wide, lane, sub)
        for i in range(k + 1, count):
            left = r_ref[pl.ds(base, LANES), pl.ds(i * LANES, LANES)]
            right = r_ref[pl.ds(base, LANES), pl.ds(i * LANES, cols - i * LANES)]
            a_ref[pl.ds(i * LANES, LANES), pl.ds(i * LANES, cols - i * LANES)] -= lax.dot_general(
                left,
                right,
                (((0,), (0,)), ((), ())),
                precision=lax.Precision.HIGHEST,
                preferred_element_type=jnp.float32,
            )


def factor(n, cols, kaula_square, pieces):
    height = len(upper_blocks(cols)) * LANES
    return pl.pallas_call(
        functools.partial(factor_kernel, n, cols),
        out_shape=jax.ShapeDtypeStruct((cols, cols), jnp.float32),
        in_specs=[pl.BlockSpec(memory_space=VMEM)] * (n + 1),
        out_specs=pl.BlockSpec(memory_space=VMEM),
        scratch_shapes=[
            pltpu.VMEM((cols, cols), jnp.float32),
            pltpu.VMEM((height, LANES), jnp.float32),
        ],
        compiler_params=pltpu.CompilerParams(vmem_limit_bytes=32 << 20),
        name="factor",
    )(kaula_square, *pieces)


def pairs(size, k):
    return [(i, i ^ k) for i in range(size)]


def swap(x, axis, k):
    return lax.ppermute(x, axis, pairs(lax.axis_size(axis), k)) if k else x


def tree_sum(terms):
    while len(terms) > 1:
        terms = [a + b for a, b in zip(terms[::2], terms[1::2])]
    return terms[0]


def body(legendre, lon_center, counts, column_index):
    n, groups = lax.axis_size("ord"), lax.axis_size("grp")
    cols_dev, rows_grp = legendre.shape
    cols = cols_dev * n
    rows_dev = rows_grp // n
    valid_rows = 3 * rows_grp // 4
    per = -(-((valid_rows + (LANES - 1) * n) // LANES) // n)
    late = max(1, per // 5)
    shape = (n, (per - late, late), rows_dev, rows_grp, 1.0 / math.sqrt(rows_grp * groups))
    order = sorted(range(1, n), key=lambda k: (-bin(k >> 1).count("1"), k)) + [0]
    early_parts, late_parts = [None] * n, [None] * n
    for k in order:
        sent = design_for(shape, k, counts, lon_center, column_index, legendre)
        early_parts[k] = swap(sent[0], "ord", k)
        late_parts[k] = swap(sent[1], "ord", k)
    before = gram(n, early_parts, [], False)
    pieces = gram(n, late_parts, before, True)
    share = tree_sum([swap(pieces[k], "ord", k) for k in range(n)])
    share = tree_sum([swap(share, "grp", k) for k in range(groups)])
    gathered = [swap(share, "ord", k) for k in range(n)]
    degree = column_index[0:1].astype(jnp.float32)
    kaula_weight = kaula_gain * (degree / NMAX) ** 2
    return factor(n, cols, kaula_weight * kaula_weight, gathered)


def solution(mesh):
    placed = (P("ord", "grp"), P("grp"), P("grp", None), P())
    return jax.shard_map(body, mesh=mesh, in_specs=placed, out_specs=P(), check_vma=False)
```

```python
import functools
import math

import jax
import jax.numpy as jnp
from jax import lax
from jax.experimental import pallas as pl
from jax.experimental.pallas import tpu as pltpu
from jax.sharding import PartitionSpec as P

NMAX = 120
LANES = 128
SUBS = 8

quarter_turn = math.pi / 2
track_span = 0.3
kaula_gain = 1.2
VMEM = pltpu.VMEM
SMEM = pltpu.SMEM


def wave_pair(x):
    turns = jnp.floor(x * (1.0 / math.pi) + 0.5)
    rest = x - turns * 3.140625
    rest = rest - turns * 9.67653589793e-4
    half = turns * 0.5
    sign = 1.0 - 4.0 * (half - jnp.floor(half))
    sq = rest * rest

    def series(powers):
        acc = None
        for power in powers:
            term = (-1.0) ** (power // 2) / math.factorial(power)
            acc = term if acc is None else acc * sq + term
        return acc

    return series((12, 10, 8, 6, 4, 2, 0)) * sign, series((13, 11, 9, 7, 5, 3, 1)) * rest * sign


def design_kernel(shape, k, counts_ref, lon_ref, index_ref, leg_ref, *refs):
    n, sizes, rows_dev, rows_grp, scaling = shape
    outs, (held, sems) = refs[:-2], refs[-2:]
    per = sum(sizes)
    blocks_dev = rows_dev // LANES
    me = lax.axis_index("ord")
    count = [counts_ref[0, r] for r in range(n)]
    ends, total = [], 0
    for r in range(n):
        total = total + lax.div(count[r] + (LANES - 1), LANES)
        ends.append(total)

    def place(want):
        slot, begin, held_rows = 0, 0, count[0]
        for r in range(n - 1):
            past = want >= ends[r]
            slot = jnp.where(past, r + 1, slot)
            begin = jnp.where(past, ends[r], begin)
            held_rows = jnp.where(past, count[r + 1], held_rows)
        inside = jnp.minimum(want - begin, blocks_dev - 1)
        valid = jnp.where(want < total, held_rows - (want - begin) * LANES, 0)
        return slot * rows_dev + inside * LANES, valid

    def copy(i, start):
        return pltpu.make_async_copy(
            leg_ref.at[:, pl.ds(start, LANES)], held.at[:, pl.ds(i * LANES, LANES)], sems.at[i]
        )

    valids = []
    for i in range(per):
        start, valid = place((me ^ k) * per + i)
        copy(i, pl.multiple_of(start, LANES)).start()
        valids.append(valid)
    rows = held.shape[0]
    wide = (rows, index_ref.shape[1])
    mine = lax.broadcasted_iota(jnp.int32, wide, 1) == lax.broadcasted_iota(jnp.int32, wide, 0) + me * rows

    def column(row):
        values = jnp.broadcast_to(index_ref[row : row + 1, :].astype(jnp.float32), wide)
        picked = jnp.sum(jnp.where(mine, values, 0.0), axis=1, keepdims=True)
        return jnp.broadcast_to(picked, (rows, LANES))

    harmonic = column(1)
    phase = column(2) * quarter_turn
    lane = lax.broadcasted_iota(jnp.int32, (SUBS, LANES), 1)
    pace = track_span / rows_grp
    along = lane.astype(jnp.float32) * pace
    tops = range(0, rows, SUBS)
    inner = [wave_pair(harmonic[top : top + SUBS] * along) for top in tops]
    begin = place((me ^ k) * per + lane)[0].astype(jnp.float32)
    longitude = lon_ref[0] + begin * pace
    outer = [
        wave_pair(harmonic[top : top + SUBS] * longitude - phase[top : top + SUBS]) for top in tops
    ]
    spots = [(out, i) for out, size in zip(outs, sizes) for i in range(size)]
    for i, (out, spot) in enumerate(spots):
        copy(i, 0).wait()
        gate = jnp.where(lane < valids[i], scaling, 0.0)
        for t, top in enumerate(tops):
            wave = lane_wide(outer[t][0], i) * inner[t][0] - lane_wide(outer[t][1], i) * inner[t][1]
            tile = held[pl.ds(top, SUBS), pl.ds(i * LANES, LANES)]
            out[pl.ds(top, SUBS), pl.ds(spot * LANES, LANES)] = tile * wave * gate


@functools.partial(jax.jit, static_argnums=(0, 1))
def design(shape, k, counts, lon_center, column_index, legendre):
    sizes, rows = shape[1], legendre.shape[0]
    elements = rows * sum(sizes) * LANES
    return pl.pallas_call(
        functools.partial(design_kernel, shape, k),
        out_shape=[jax.ShapeDtypeStruct((rows, size * LANES), jnp.float32) for size in sizes],
        in_specs=[
            pl.BlockSpec(memory_space=SMEM),
            pl.BlockSpec(memory_space=SMEM),
            pl.BlockSpec(memory_space=VMEM),
            pl.BlockSpec(memory_space=pltpu.HBM),
        ],
        out_specs=[pl.BlockSpec(memory_space=VMEM)] * len(sizes),
        scratch_shapes=[
            pltpu.VMEM((rows, sum(sizes) * LANES), jnp.float32),
            pltpu.SemaphoreType.DMA((sum(sizes),)),
        ],
        compiler_params=pltpu.CompilerParams(vmem_limit_bytes=56 << 20),
        cost_estimate=pl.CostEstimate(flops=8 * elements, bytes_accessed=8 * elements, transcendentals=0),
        name="design",
    )(counts, lon_center, column_index, legendre)


def lane_wide(x, j):
    return jnp.broadcast_to(x[:, j : j + 1], (SUBS, LANES))


def upper_blocks(cols):
    nb = cols // LANES
    return [(i, j) for i in range(nb) for j in range(i, nb)]


def gram_kernel(n, cols, tile, first, last, *refs):
    ins, refs = refs[:n], refs[n:]
    before = None
    if not first:
        before, refs = refs[0], refs[1:]
    outs, scratch = refs[: n if last else 1], refs[n if last else 1 :]
    high, low = scratch[:2]
    acc = scratch[2] if last else outs[0]
    me = lax.axis_index("ord")
    each, rows = ins[0].shape

    def times(a, b):
        return lax.dot_general(a, b, (((1,), (1,)), ((), ())), preferred_element_type=jnp.float32)

    tall = min(256, cols)
    for s in range(rows // tile):
        for k in range(n):
            part = ins[k][:, pl.ds(s * tile, tile)]
            at = pl.ds(pl.multiple_of((me ^ k) * each, each), each)
            top = part.astype(jnp.bfloat16)
            high[s % 2, at, :] = top
            low[s % 2, at, :] = (part - top.astype(jnp.float32)).astype(jnp.bfloat16)
        for i in range(0, cols, tall):
            hi, lo = high[s % 2, pl.ds(i, tall), :], low[s % 2, pl.ds(i, tall), :]
            his, los = high[s % 2, pl.ds(i, cols - i), :], low[s % 2, pl.ds(i, cols - i), :]
            at = (pl.ds(i, tall), pl.ds(i, cols - i))
            here = times(hi, his) + (times(hi, los) + times(lo, his))
            if s:
                acc[at] += here
            else:
                acc[at] = here if first else before[at] + here

    if last:
        packed = scratch[3]
        for t, (i, j) in enumerate(upper_blocks(cols)):
            packed[pl.ds(t * LANES, LANES), :] = acc[pl.ds(i * LANES, LANES), pl.ds(j * LANES, LANES)]
        piece = packed.shape[0] // n
        for k in range(n):
            outs[k][...] = packed[pl.ds(pl.multiple_of((me ^ k) * piece, SUBS), piece), :]


def gram(n, parts, before, last):
    each, rows = parts[0].shape
    cols = each * n
    tile = 640 if rows % 640 == 0 else LANES
    height = len(upper_blocks(cols)) * LANES
    scratch = [pltpu.VMEM((2, cols, tile), jnp.bfloat16)] * 2
    if last:
        out_shape = [jax.ShapeDtypeStruct((height // n, LANES), jnp.float32)] * n
        scratch += [pltpu.VMEM((cols, cols), jnp.float32), pltpu.VMEM((height, LANES), jnp.float32)]
    else:
        out_shape = [jax.ShapeDtypeStruct((cols, cols), jnp.float32)]
    return pl.pallas_call(
        functools.partial(gram_kernel, n, cols, tile, not before, last),
        out_shape=out_shape,
        in_specs=[pl.BlockSpec(memory_space=VMEM)] * (n + len(before)),
        out_specs=[pl.BlockSpec(memory_space=VMEM)] * len(out_shape),
        scratch_shapes=scratch,
        compiler_params=pltpu.CompilerParams(vmem_limit_bytes=32 << 20),
        cost_estimate=pl.CostEstimate(
            flops=6 * cols * cols * rows, bytes_accessed=4 * cols * rows, transcendentals=0
        ),
        name="gram",
    )(*parts, *before)


def row_wide(ref, row, column):
    return jnp.broadcast_to(ref[pl.ds(row, 1), pl.ds(column, LANES)], (SUBS, LANES))


def factor_panel(a_ref, r_ref, u_ref, t_ref, base, p, wide, lane, sub, columns):
    groups = LANES // SUBS
    row0, c0 = base + SUBS * p, SUBS * p
    slot = (p % 2) * SUBS * SUBS
    if columns is None:
        own = a_ref[pl.ds(row0, SUBS), pl.ds(base, LANES)]
        columns = [lane_wide(own, c0 + j) for j in range(SUBS)]
    for j in range(SUBS):
        u_ref[pl.ds(slot + SUBS * j, SUBS), :] = columns[j]
    d = {(i, j): row_wide(u_ref, slot + SUBS * j + i, 0) for j in range(SUBS) for i in range(j + 1)}
    inv, up = [None] * SUBS, {}
    for i in range(SUBS):
        inv[i] = lax.rsqrt(d[i, i])
        for j in range(i + 1, SUBS):
            up[i, j] = d[i, j] * inv[i]
        for a in range(i + 1, SUBS):
            for b in range(a, SUBS):
                d[a, b] = d[a, b] - up[i, a] * up[i, b]
    coef, following = [], None
    if p + 1 < groups:
        below = a_ref[pl.ds(row0 + SUBS, SUBS), pl.ds(base, LANES)]
        for j in range(SUBS):
            acc = lane_wide(below, c0 + j)
            for i in range(j):
                acc = acc - up[i, j] * coef[i]
            coef.append(acc * inv[j])
            t_ref[pl.ds(slot + SUBS * j, SUBS), :] = coef[j]
        following = [
            lane_wide(below, c0 + SUBS + b)
            - tree_sum([coef[j] * row_wide(t_ref, slot + SUBS * j + b, 0) for j in range(SUBS)])
            for b in range(SUBS)
        ]
    done = [[None] * SUBS for _ in range(wide)]
    for w in range(wide):
        for i in range(SUBS):
            acc = row_wide(a_ref, row0 + i, base + LANES * w)
            for j in range(i):
                acc = acc - up[j, i] * done[w][j]
            done[w][i] = acc * inv[i]

    def update(g, coef, rows):
        for w in range(wide):
            at = (pl.ds(base + SUBS * g, SUBS), pl.ds(base + LANES * w, LANES))
            a_ref[at] = a_ref[at] - tree_sum([coef[j] * rows[w][j] for j in range(SUBS)])

    if p + 1 < groups:
        update(p + 1, coef, done)
    if p + 2 < groups:
        solved = [[None] * SUBS for _ in range(wide)]
        for w in range(wide):
            for i in range(SUBS - 1, -1, -1):
                acc = done[w][i]
                for j in range(i + 1, SUBS):
                    acc = acc - up[i, j] * solved[w][j]
                solved[w][i] = acc * inv[i]
        for g in range(p + 2, groups):
            below = a_ref[pl.ds(base + SUBS * g, SUBS), pl.ds(base, LANES)]
            update(g, [lane_wide(below, c0 + j) for j in range(SUBS)], solved)
    for w in range(wide):
        out = done[w][0]
        for i in range(1, SUBS):
            out = jnp.where(sub == i, done[w][i], out)
        if w == 0:
            out = jnp.where(lane >= sub + c0, out, 0.0)
        r_ref[pl.ds(row0, SUBS), pl.ds(base + LANES * w, LANES)] = out
    return following


def factor_kernel(n, cols, kaula_ref, *refs):
    ins, (r_ref, a_ref, packed, u_ref, t_ref) = refs[:n], refs[n:]
    me = lax.axis_index("ord")
    piece = packed.shape[0] // n
    for k in range(n):
        packed[pl.ds(pl.multiple_of((me ^ k) * piece, SUBS), piece), :] = ins[k][...]
    square = (LANES, LANES)
    diag = lax.broadcasted_iota(jnp.int32, square, 0) == lax.broadcasted_iota(jnp.int32, square, 1)
    for t, (i, j) in enumerate(upper_blocks(cols)):
        block = packed[pl.ds(t * LANES, LANES), :]
        if i == j:
            block = block + jnp.where(diag, kaula_ref[:, pl.ds(i * LANES, LANES)], 0.0)
        a_ref[pl.ds(i * LANES, LANES), pl.ds(j * LANES, LANES)] = block
    lane = lax.broadcasted_iota(jnp.int32, (SUBS, LANES), 1)
    sub = lax.broadcasted_iota(jnp.int32, (SUBS, LANES), 0)
    count = cols // LANES
    for k in range(count):
        base, wide = k * LANES, count - k
        if base:
            r_ref[pl.ds(base, LANES), pl.ds(0, base)] = jnp.zeros((LANES, base), jnp.float32)
        columns = None
        for p in range(LANES // SUBS):
            columns = factor_panel(a_ref, r_ref, u_ref, t_ref, base, p, wide, lane, sub, columns)
        for i in range(k + 1, count):
            left = r_ref[pl.ds(base, LANES), pl.ds(i * LANES, LANES)]
            right = r_ref[pl.ds(base, LANES), pl.ds(i * LANES, cols - i * LANES)]
            a_ref[pl.ds(i * LANES, LANES), pl.ds(i * LANES, cols - i * LANES)] -= lax.dot_general(
                left,
                right,
                (((0,), (0,)), ((), ())),
                precision=lax.Precision.HIGHEST,
                preferred_element_type=jnp.float32,
            )


def factor(n, cols, kaula_square, pieces):
    height = len(upper_blocks(cols)) * LANES
    return pl.pallas_call(
        functools.partial(factor_kernel, n, cols),
        out_shape=jax.ShapeDtypeStruct((cols, cols), jnp.float32),
        in_specs=[pl.BlockSpec(memory_space=VMEM)] * (n + 1),
        out_specs=pl.BlockSpec(memory_space=VMEM),
        scratch_shapes=[
            pltpu.VMEM((cols, cols), jnp.float32),
            pltpu.VMEM((height, LANES), jnp.float32),
            pltpu.VMEM((2 * SUBS * SUBS, LANES), jnp.float32),
            pltpu.VMEM((2 * SUBS * SUBS, LANES), jnp.float32),
        ],
        compiler_params=pltpu.CompilerParams(vmem_limit_bytes=32 << 20),
        name="factor",
    )(kaula_square, *pieces)


def pairs(size, k):
    return [(i, i ^ k) for i in range(size)]


def swap(x, axis, k):
    return lax.ppermute(x, axis, pairs(lax.axis_size(axis), k)) if k else x


def tree_sum(terms):
    while len(terms) > 1:
        terms = [a + b for a, b in zip(terms[::2], terms[1::2])]
    return terms[0]


def body(legendre, lon_center, counts, column_index):
    n, groups = lax.axis_size("ord"), lax.axis_size("grp")
    cols_dev, rows_grp = legendre.shape
    cols = cols_dev * n
    rows_dev = rows_grp // n
    valid_rows = 3 * rows_grp // 4
    per = -(-((valid_rows + (LANES - 1) * n) // LANES) // n)
    late = max(1, per // 5)
    shape = (n, (per - late, late), rows_dev, rows_grp, 1.0 / math.sqrt(rows_grp * groups))
    order = sorted(range(1, n), key=lambda k: (-bin(k >> 1).count("1"), k)) + [0]
    early_parts, late_parts = [None] * n, [None] * n
    for k in order:
        early_parts[k], late_parts[k] = design(shape, k, counts, lon_center, column_index, legendre)
        early_parts[k] = swap(early_parts[k], "ord", k)
    gate = order[1]
    early_parts[gate], late_parts = lax.optimization_barrier((early_parts[gate], late_parts))
    late_parts = [swap(late_parts[k], "ord", k) for k in range(n)]
    before = gram(n, early_parts, [], False)
    pieces = gram(n, late_parts, before, True)
    share = tree_sum([swap(pieces[k], "ord", k) for k in range(n)])
    share = tree_sum([swap(share, "grp", k) for k in range(groups)])
    gathered = [swap(share, "ord", k) for k in range(n)]
    degree = column_index[0:1].astype(jnp.float32)
    kaula_weight = kaula_gain * (degree / NMAX) ** 2
    return factor(n, cols, kaula_weight * kaula_weight, gathered)


def solution(mesh):
    placed = (P("ord", "grp"), P("grp"), P("grp", None), P())
    return jax.shard_map(body, mesh=mesh, in_specs=placed, out_specs=P(), check_vma=False)
```

```python
import functools
import math

import jax
import jax.numpy as jnp
from jax import lax
from jax.experimental import pallas as pl
from jax.experimental.pallas import tpu as pltpu
from jax.sharding import PartitionSpec as P

NMAX = 120
LANES = 128
SUBS = 8

quarter_turn = math.pi / 2
track_span = 0.3
kaula_gain = 1.2
VMEM = pltpu.VMEM
SMEM = pltpu.SMEM


def wave_pair(x):
    turns = jnp.floor(x * (1.0 / math.pi) + 0.5)
    rest = x - turns * 3.140625
    rest = rest - turns * 9.67653589793e-4
    half = turns * 0.5
    sign = 1.0 - 4.0 * (half - jnp.floor(half))
    sq = rest * rest

    def series(powers):
        acc = None
        for power in powers:
            term = (-1.0) ** (power // 2) / math.factorial(power)
            acc = term if acc is None else acc * sq + term
        return acc

    return series((12, 10, 8, 6, 4, 2, 0)) * sign, series((13, 11, 9, 7, 5, 3, 1)) * rest * sign


class Blocks:
    def __init__(self, shape, counts_ref):
        self.n, self.per, self.rows_dev = shape[:3]
        self.ends, self.rest, self.rest_starts, self.rest_places = [], [], [], []
        total, rest_total = 0, 0
        for r in range(self.n):
            count = counts_ref[0, r]
            full = lax.div(count, LANES)
            total = total + full
            self.ends.append(total)
            self.rest.append(count - full * LANES)
            self.rest_starts.append(rest_total)
            self.rest_places.append(r * self.rows_dev + jnp.minimum(full * LANES, self.rows_dev - LANES))
            rest_total = rest_total + self.rest[r]
        self.packed = lax.div(rest_total, LANES)

    def first(self, dest):
        return dest * self.per - jnp.minimum(dest, self.packed)

    def place(self, want):
        slot, begin = 0, 0
        for r in range(self.n - 1):
            past = want >= self.ends[r]
            slot = jnp.where(past, r + 1, slot)
            begin = jnp.where(past, self.ends[r], begin)
        return slot * self.rows_dev + jnp.minimum((want - begin) * LANES, self.rows_dev - LANES)


def over(count, n, step):
    def run(i, _):
        step(i)
        return 0

    lax.fori_loop(0, count, run, 0, unroll=count if n <= 8 else 1)


def pick_kernel(shape, k, size, counts_ref, leg_ref, out_ref, sems):
    blocks = Blocks(shape, counts_ref)
    dest = lax.axis_index("ord") ^ k

    def copy(i, start):
        here = pl.ds(pl.multiple_of(i * LANES, LANES), LANES)
        return pltpu.make_async_copy(leg_ref.at[:, pl.ds(start, LANES)], out_ref.at[:, here], sems.at[i])

    def send(i):
        copy(i, pl.multiple_of(blocks.place(blocks.first(dest) + i), LANES)).start()

    def wait(i):
        copy(i, 0).wait()

    over(size, blocks.n, send)
    over(size, blocks.n, wait)


@functools.partial(jax.jit, static_argnums=(0, 1, 2))
def pick(shape, k, size, counts, legendre):
    rows = legendre.shape[0]
    elements = rows * size * LANES
    return pl.pallas_call(
        functools.partial(pick_kernel, shape, k, size),
        out_shape=jax.ShapeDtypeStruct((rows, size * LANES), jnp.float32),
        in_specs=[pl.BlockSpec(memory_space=SMEM), pl.BlockSpec(memory_space=pltpu.HBM)],
        out_specs=pl.BlockSpec(memory_space=VMEM),
        scratch_shapes=[pltpu.SemaphoreType.DMA((size,))],
        compiler_params=pltpu.CompilerParams(vmem_limit_bytes=56 << 20),
        cost_estimate=pl.CostEstimate(flops=8 * elements, bytes_accessed=8 * elements, transcendentals=0),
        name="pick",
    )(counts, legendre)


def inner_tables(shape, harmonic, tops):
    along = lax.broadcasted_iota(jnp.int32, (SUBS, LANES), 1).astype(jnp.float32) * (track_span / shape[3])
    pairs_of = [wave_pair(harmonic[top : top + SUBS] * along) for top in tops]
    return [(c * shape[4], s * shape[4]) for c, s in pairs_of]


def outer_tables(shape, lon, begin, harmonic, phase, tops):
    longitude = lon + begin.astype(jnp.float32) * (track_span / shape[3])
    return [wave_pair(harmonic[top : top + SUBS] * longitude - phase[top : top + SUBS]) for top in tops]


def wave(outer, inner, i):
    return lane_wide(outer[0], i) * inner[0] - lane_wide(outer[1], i) * inner[1]


def wide_columns(columns):
    rows = columns.shape[0]
    harmonic = jnp.broadcast_to(columns[:, 0:1], (rows, LANES))
    return harmonic, jnp.broadcast_to(columns[:, 1:2] * quarter_turn, (rows, LANES))


def design_kernel(shape, ks, first, size, counts_ref, lon_ref, cols_ref, leg_ref, *refs):
    blocks = Blocks(shape, counts_ref)
    n, last = blocks.n, first + size == blocks.per
    outs, (held, left, table, sems, left_sems) = refs[: len(ks)], refs[len(ks) :]
    me = lax.axis_index("ord")

    def origin(k):
        return blocks.first(me ^ k) + first

    def copy(spot, start):
        here = pl.ds(pl.multiple_of(spot * LANES, LANES), LANES)
        return pltpu.make_async_copy(leg_ref.at[:, pl.ds(start, LANES)], held.at[:, here], sems.at[spot])

    def copy_rest(r, start):
        here = pl.ds(r * LANES, LANES)
        return pltpu.make_async_copy(leg_ref.at[:, pl.ds(start, LANES)], left.at[:, here], left_sems.at[r])

    def send(i):
        for q, k in enumerate(ks):
            copy(q * size + i, pl.multiple_of(blocks.place(origin(k) + i), LANES)).start()

    over(size, n, send)
    for r in range(n if last else 0):
        copy_rest(r, pl.multiple_of(blocks.rest_places[r], LANES)).start()
        table[0, r] = blocks.rest[r]
        table[1, r] = blocks.rest_starts[r]
    rows = held.shape[0]
    tops = range(0, rows, SUBS)
    lane = lax.broadcasted_iota(jnp.int32, (SUBS, LANES), 1)
    harmonic, phase = wide_columns(cols_ref[...])
    inner = inner_tables(shape, harmonic, tops)
    begin = jnp.zeros_like(lane)
    for r in range(n):
        begin = jnp.where(lane == r, blocks.rest_places[r], begin)
    outer = outer_tables(shape, lon_ref[0], begin, harmonic, phase, tops) if last else None
    for r in range(n if last else 0):
        copy_rest(r, 0).wait()
        for t, top in enumerate(tops):
            at = (pl.ds(top, SUBS), pl.ds(r * LANES, LANES))
            left[at] = jnp.where(lane < blocks.rest[r], left[at] * wave(outer[t], inner[t], r), 0.0)
    whole_lane = lax.broadcasted_iota(jnp.int32, (rows, LANES), 1)
    for q, k in enumerate(ks):
        outer = outer_tables(shape, lon_ref[0], blocks.place(origin(k) + lane), harmonic, phase, tops)
        for i in range(size):
            copy(q * size + i, 0).wait()
            for t, top in enumerate(tops):
                tile = held[pl.ds(top, SUBS), pl.ds((q * size + i) * LANES, LANES)]
                outs[q][pl.ds(top, SUBS), pl.ds(i * LANES, LANES)] = tile * wave(outer[t], inner[t], i)
        if not last:
            continue

        @pl.when((me ^ k) < blocks.packed)
        def _(q=q, k=k):
            here = pl.ds((size - 1) * LANES, LANES)
            outs[q][:, here] = jnp.zeros((rows, LANES), jnp.float32)

            def add(r, _):
                many = table[0, r]
                shift = table[1, r] - (me ^ k) * LANES

                @pl.when((shift < LANES) & (shift + many > 0))
                def _():
                    spot = whole_lane - shift
                    tile = left[:, pl.ds(pl.multiple_of(r * LANES, LANES), LANES)]
                    rolled = pltpu.roll(tile, lax.rem(shift + LANES, LANES), 1)
                    outs[q][:, here] += jnp.where((spot >= 0) & (spot < many), rolled, 0.0)

                return 0

            lax.fori_loop(0, n, add, 0)


@functools.partial(jax.jit, static_argnums=(0, 1, 2, 3))
def design(shape, ks, first, size, counts, lon_center, own, legendre):
    n, rows, many = shape[0], legendre.shape[0], len(ks) * size
    elements = rows * many * LANES
    return pl.pallas_call(
        functools.partial(design_kernel, shape, ks, first, size),
        out_shape=[jax.ShapeDtypeStruct((rows, size * LANES), jnp.float32)] * len(ks),
        in_specs=[
            pl.BlockSpec(memory_space=SMEM),
            pl.BlockSpec(memory_space=SMEM),
            pl.BlockSpec(memory_space=VMEM),
            pl.BlockSpec(memory_space=pltpu.HBM),
        ],
        out_specs=[pl.BlockSpec(memory_space=VMEM)] * len(ks),
        scratch_shapes=[
            pltpu.VMEM((rows, many * LANES), jnp.float32),
            pltpu.VMEM((rows, n * LANES), jnp.float32),
            pltpu.SMEM((2, n), jnp.int32),
            pltpu.SemaphoreType.DMA((many,)),
            pltpu.SemaphoreType.DMA((n,)),
        ],
        compiler_params=pltpu.CompilerParams(vmem_limit_bytes=56 << 20),
        cost_estimate=pl.CostEstimate(flops=8 * elements, bytes_accessed=8 * elements, transcendentals=0),
        name="design",
    )(counts, lon_center, own, legendre)


def lane_wide(x, j):
    return jnp.broadcast_to(x[:, j : j + 1], (SUBS, LANES))


def upper_blocks(cols):
    nb = cols // LANES
    return [(i, j) for i in range(nb) for j in range(i, nb)]


def gram_terms(n, cols, tile, ins, high, low, value, add):
    me = lax.axis_index("ord")
    each, rows = ins[0].shape

    def times(a, b):
        return lax.dot_general(a, b, (((1,), (1,)), ((), ())), preferred_element_type=jnp.float32)

    tall = min(256, cols)
    for s in range(rows // tile):
        for k in range(n):
            begin = pl.multiple_of((me ^ k) * each, each)
            value(k, s, begin, ins[k], high.at[s % 2], low.at[s % 2])
        for i in range(0, cols, tall):
            hi, lo = high[s % 2, pl.ds(i, tall), :], low[s % 2, pl.ds(i, tall), :]
            his, los = high[s % 2, pl.ds(i, cols - i), :], low[s % 2, pl.ds(i, cols - i), :]
            add(s, (pl.ds(i, tall), pl.ds(i, cols - i)), times(hi, his) + (times(hi, los) + times(lo, his)))


def split(x):
    top = x.astype(jnp.bfloat16)
    return top, (x - top.astype(jnp.float32)).astype(jnp.bfloat16)


def early_kernel(shape, cols, tile, raw, counts_ref, lon_ref, cols_ref, *refs):
    n = shape[0]
    ins, (acc, high, low, inner_ref, outer_ref) = refs[:n], refs[n:]
    blocks = Blocks(shape, counts_ref)
    me = lax.axis_index("ord")
    each = cols // n
    tops = range(0, each, SUBS)
    lane = lax.broadcasted_iota(jnp.int32, (SUBS, LANES), 1)
    begins = blocks.place(blocks.first(me) + lane)
    for q, k in enumerate(raw):
        harmonic, phase = wide_columns(cols_ref[pl.ds(pl.multiple_of((me ^ k) * each, each), each), :])
        inner = inner_tables(shape, harmonic, tops)
        outer = outer_tables(shape, lon_ref[0], begins, harmonic, phase, tops)
        for t, top in enumerate(tops):
            for half in range(2):
                inner_ref[half, pl.ds(q * each + top, SUBS), :] = inner[t][half]
                outer_ref[half, pl.ds(q * each + top, SUBS), :] = outer[t][half]
    step = 2 * SUBS

    def value(k, s, begin, part, high_ref, low_ref):
        if k not in raw:
            at = pl.ds(begin, each)
            high_ref[at, :], low_ref[at, :] = split(part[:, pl.ds(s * tile, tile)])
            return
        for top in range(0, each, step):
            there = pl.ds(raw.index(k) * each + top, step)
            inside = [inner_ref[half, there, :] for half in range(2)]
            outside = [outer_ref[half, there, :] for half in range(2)]
            for i in range(tile // LANES):
                b = s * (tile // LANES) + i
                c, d = (jnp.broadcast_to(x[:, b : b + 1], (step, LANES)) for x in outside)
                x = part[pl.ds(top, step), pl.ds(b * LANES, LANES)] * (c * inside[0] - d * inside[1])
                here = (pl.ds(pl.multiple_of(begin + top, step), step), pl.ds(i * LANES, LANES))
                high_ref[here], low_ref[here] = split(x)

    def add(s, at, block):
        acc[at] = acc[at] + block if s else block

    gram_terms(n, cols, tile, ins, high, low, value, add)


def late_kernel(n, cols, tile, *refs):
    ins, (before, keep, give, high, low, acc, packed) = refs[:n], refs[n:]
    me = lax.axis_index("ord")
    each = cols // n

    def value(k, s, begin, part, high_ref, low_ref):
        at = pl.ds(begin, each)
        high_ref[at, :], low_ref[at, :] = split(part[:, pl.ds(s * tile, tile)])

    def add(s, at, block):
        acc[at] = (acc[at] if s else before[at]) + block

    gram_terms(n, cols, tile, ins, high, low, value, add)
    for t, (i, j) in enumerate(upper_blocks(cols)):
        packed[pl.ds(t * LANES, LANES), :] = acc[pl.ds(i * LANES, LANES), pl.ds(j * LANES, LANES)]
    piece = packed.shape[0] // n
    for k in range(n):
        there = packed[pl.ds(pl.multiple_of((me ^ k) * piece, SUBS), piece), :]
        (give if k % 2 else keep)[pl.ds(k // 2 * piece, piece), :] = there


def tile_of(rows):
    return max(t for t in range(LANES, 641, LANES) if rows % t == 0)


def early_gram(shape, raw, counts, lon_center, columns, parts):
    n = shape[0]
    each, rows = parts[0].shape
    cols, tile = each * n, tile_of(rows)
    vmem = pl.BlockSpec(memory_space=VMEM)
    return pl.pallas_call(
        functools.partial(early_kernel, shape, cols, tile, raw),
        out_shape=jax.ShapeDtypeStruct((cols, cols), jnp.float32),
        in_specs=[pl.BlockSpec(memory_space=SMEM)] * 2 + [vmem] * (n + 1),
        out_specs=vmem,
        scratch_shapes=[pltpu.VMEM((2, cols, tile), jnp.bfloat16)] * 2
        + [pltpu.VMEM((2, len(raw) * each, LANES), jnp.float32)] * 2,
        compiler_params=pltpu.CompilerParams(vmem_limit_bytes=32 << 20),
        cost_estimate=pl.CostEstimate(flops=0, bytes_accessed=0, transcendentals=0),
        name="gram",
    )(counts, lon_center, columns, *parts)


def late_gram(n, parts, before):
    each, rows = parts[0].shape
    cols, tile = each * n, tile_of(rows)
    height = len(upper_blocks(cols)) * LANES
    vmem = pl.BlockSpec(memory_space=VMEM)
    return pl.pallas_call(
        functools.partial(late_kernel, n, cols, tile),
        out_shape=[jax.ShapeDtypeStruct((height // 2, LANES), jnp.float32)] * 2,
        in_specs=[vmem] * (n + 1),
        out_specs=[vmem] * 2,
        scratch_shapes=[pltpu.VMEM((2, cols, tile), jnp.bfloat16)] * 2
        + [pltpu.VMEM((cols, cols), jnp.float32), pltpu.VMEM((height, LANES), jnp.float32)],
        compiler_params=pltpu.CompilerParams(vmem_limit_bytes=32 << 20),
        cost_estimate=pl.CostEstimate(
            flops=6 * cols * cols * rows, bytes_accessed=4 * cols * rows, transcendentals=0
        ),
        name="gram_late",
    )(*parts, before)


def row_wide(ref, row, column):
    return jnp.broadcast_to(ref[pl.ds(row, 1), pl.ds(column, LANES)], (SUBS, LANES))


def factor_panel(a_ref, r_ref, u_ref, t_ref, base, p, wide, lane, sub, columns):
    groups = LANES // SUBS
    row0, c0 = base + SUBS * p, SUBS * p
    slot = (p % 2) * SUBS * SUBS
    if columns is None:
        own = a_ref[pl.ds(row0, SUBS), pl.ds(base, LANES)]
        columns = [lane_wide(own, c0 + j) for j in range(SUBS)]
    for j in range(SUBS):
        u_ref[pl.ds(slot + SUBS * j, SUBS), :] = columns[j]
    d = {(i, j): row_wide(u_ref, slot + SUBS * j + i, 0) for j in range(SUBS) for i in range(j + 1)}
    inv, up = [None] * SUBS, {}
    for i in range(SUBS):
        inv[i] = lax.rsqrt(d[i, i])
        for j in range(i + 1, SUBS):
            up[i, j] = d[i, j] * inv[i]
        for a in range(i + 1, SUBS):
            for b in range(a, SUBS):
                d[a, b] = d[a, b] - up[i, a] * up[i, b]
    coef, following = [], None
    if p + 1 < groups:
        below = a_ref[pl.ds(row0 + SUBS, SUBS), pl.ds(base, LANES)]
        for j in range(SUBS):
            acc = lane_wide(below, c0 + j)
            for i in range(j):
                acc = acc - up[i, j] * coef[i]
            coef.append(acc * inv[j])
            t_ref[pl.ds(slot + SUBS * j, SUBS), :] = coef[j]
        following = [
            lane_wide(below, c0 + SUBS + b)
            - tree_sum([coef[j] * row_wide(t_ref, slot + SUBS * j + b, 0) for j in range(SUBS)])
            for b in range(SUBS)
        ]
    done = [[None] * SUBS for _ in range(wide)]
    for w in range(wide):
        for i in range(SUBS):
            acc = row_wide(a_ref, row0 + i, base + LANES * w)
            for j in range(i):
                acc = acc - up[j, i] * done[w][j]
            done[w][i] = acc * inv[i]

    def update(g, coef, rows):
        for w in range(wide):
            at = (pl.ds(base + SUBS * g, SUBS), pl.ds(base + LANES * w, LANES))
            a_ref[at] = a_ref[at] - tree_sum([coef[j] * rows[w][j] for j in range(SUBS)])

    if p + 1 < groups:
        update(p + 1, coef, done)
    if p + 2 < groups:
        solved = [[None] * SUBS for _ in range(wide)]
        for w in range(wide):
            for i in range(SUBS - 1, -1, -1):
                acc = done[w][i]
                for j in range(i + 1, SUBS):
                    acc = acc - up[i, j] * solved[w][j]
                solved[w][i] = acc * inv[i]
        for g in range(p + 2, groups):
            below = a_ref[pl.ds(base + SUBS * g, SUBS), pl.ds(base, LANES)]
            update(g, [lane_wide(below, c0 + j) for j in range(SUBS)], solved)
    for w in range(wide):
        out = done[w][0]
        for i in range(1, SUBS):
            out = jnp.where(sub == i, done[w][i], out)
        if w == 0:
            out = jnp.where(lane >= sub + c0, out, 0.0)
        r_ref[pl.ds(row0, SUBS), pl.ds(base + LANES * w, LANES)] = out
    return following


def factor_kernel(n, cols, kaula_ref, *refs):
    ins, (r_ref, a_ref, packed, u_ref, t_ref) = refs[:n], refs[n:]
    me = lax.axis_index("ord")
    piece = packed.shape[0] // n
    for k in range(n):
        packed[pl.ds(pl.multiple_of((me ^ k) * piece, SUBS), piece), :] = ins[k][...]
    square = (LANES, LANES)
    diag = lax.broadcasted_iota(jnp.int32, square, 0) == lax.broadcasted_iota(jnp.int32, square, 1)
    for t, (i, j) in enumerate(upper_blocks(cols)):
        block = packed[pl.ds(t * LANES, LANES), :]
        if i == j:
            block = block + jnp.where(diag, kaula_ref[:, pl.ds(i * LANES, LANES)], 0.0)
        a_ref[pl.ds(i * LANES, LANES), pl.ds(j * LANES, LANES)] = block
    lane = lax.broadcasted_iota(jnp.int32, (SUBS, LANES), 1)
    sub = lax.broadcasted_iota(jnp.int32, (SUBS, LANES), 0)
    count = cols // LANES
    for k in range(count):
        base, wide = k * LANES, count - k
        if base:
            r_ref[pl.ds(base, LANES), pl.ds(0, base)] = jnp.zeros((LANES, base), jnp.float32)
        columns = None
        for p in range(LANES // SUBS):
            columns = factor_panel(a_ref, r_ref, u_ref, t_ref, base, p, wide, lane, sub, columns)
        for i in range(k + 1, count):
            left = r_ref[pl.ds(base, LANES), pl.ds(i * LANES, LANES)]
            right = r_ref[pl.ds(base, LANES), pl.ds(i * LANES, cols - i * LANES)]
            a_ref[pl.ds(i * LANES, LANES), pl.ds(i * LANES, cols - i * LANES)] -= lax.dot_general(
                left,
                right,
                (((0,), (0,)), ((), ())),
                precision=lax.Precision.HIGHEST,
                preferred_element_type=jnp.float32,
            )


def factor(n, cols, kaula_square, pieces):
    height = len(upper_blocks(cols)) * LANES
    return pl.pallas_call(
        functools.partial(factor_kernel, n, cols),
        out_shape=jax.ShapeDtypeStruct((cols, cols), jnp.float32),
        in_specs=[pl.BlockSpec(memory_space=VMEM)] * (n + 1),
        out_specs=pl.BlockSpec(memory_space=VMEM),
        scratch_shapes=[
            pltpu.VMEM((cols, cols), jnp.float32),
            pltpu.VMEM((height, LANES), jnp.float32),
            pltpu.VMEM((2 * SUBS * SUBS, LANES), jnp.float32),
            pltpu.VMEM((2 * SUBS * SUBS, LANES), jnp.float32),
        ],
        compiler_params=pltpu.CompilerParams(vmem_limit_bytes=32 << 20),
        name="factor",
    )(kaula_square, *pieces)


def pairs(size, k):
    return [(i, i ^ k) for i in range(size)]


def swap(x, axis, k):
    return lax.ppermute(x, axis, pairs(lax.axis_size(axis), k)) if k else x


def tree_sum(terms):
    while len(terms) > 1:
        terms = [a + b for a, b in zip(terms[::2], terms[1::2])]
    return terms[0]


def body(legendre, lon_center, counts, column_index):
    n, groups = lax.axis_size("ord"), lax.axis_size("grp")
    cols_dev, rows_grp = legendre.shape
    cols = cols_dev * n
    rows_dev = rows_grp // n
    valid_rows = 3 * rows_grp // 4
    per = valid_rows // LANES // n
    late = max(1, per // 6)
    early = per - late
    shape = (n, per, rows_dev, rows_grp, 1.0 / math.sqrt(rows_grp * groups))
    columns = column_index[1:3].astype(jnp.float32).T
    own = lax.dynamic_slice_in_dim(columns, lax.axis_index("ord") * cols_dev, cols_dev, 0)
    far = sorted(range(2, n), key=lambda k: (-bin(k >> 1).count("1"), k & 1, k))
    raw = (far[0], far[1], 1, far[2], far[3])
    early_parts = [None] * n
    for k in raw:
        early_parts[k] = swap(pick(shape, k, early, counts, legendre), "ord", k)
    early_parts[1], now = lax.optimization_barrier((early_parts[1], counts))
    for k in far[4:5] + [0] + far[5:]:
        part = design(shape, (k,), 0, early, now, lon_center, own, legendre)[0]
        part, now = lax.optimization_barrier((part, now))
        early_parts[k] = swap(part, "ord", k)
    late_parts = design(shape, tuple(range(n)), early, late, now, lon_center, own, legendre)
    late_parts = [swap(late_parts[k], "ord", k) for k in range(n)]
    before = early_gram(shape, raw, counts, lon_center, columns, early_parts)
    keep, give = late_gram(n, late_parts, before)
    half = (keep + swap(give, "ord", 1)).reshape(n // 2, -1, LANES)
    share = tree_sum([swap(half[c], "ord", 2 * c) for c in reversed(range(n // 2))])
    share = tree_sum([swap(share, "grp", k) for k in reversed(range(groups))])
    gathered = []
    for c in range(n // 2):
        there = swap(share, "ord", 2 * c)
        gathered += [there, swap(there, "ord", 1)]
    degree = column_index[0:1].astype(jnp.float32)
    kaula_weight = kaula_gain * (degree / NMAX) ** 2
    return factor(n, cols, kaula_weight * kaula_weight, gathered)


def solution(mesh):
    placed = (P("ord", "grp"), P("grp"), P("grp", None), P())
    return jax.shard_map(body, mesh=mesh, in_specs=placed, out_specs=P(), check_vma=False)
```

```python
import functools
import math

import jax
import jax.numpy as jnp
from jax import lax
from jax.experimental import pallas as pl
from jax.experimental.pallas import tpu as pltpu
from jax.sharding import PartitionSpec as P

NMAX = 120
LANES = 128
SUBS = 8

quarter_turn = math.pi / 2
track_span = 0.3
kaula_gain = 1.2
VMEM = pltpu.VMEM
SMEM = pltpu.SMEM


def wave_pair(x):
    turns = jnp.floor(x * (1.0 / math.pi) + 0.5)
    rest = x - turns * 3.140625
    rest = rest - turns * 9.67653589793e-4
    half = turns * 0.5
    sign = 1.0 - 4.0 * (half - jnp.floor(half))
    sq = rest * rest

    def series(powers):
        acc = None
        for power in powers:
            term = (-1.0) ** (power // 2) / math.factorial(power)
            acc = term if acc is None else acc * sq + term
        return acc

    return series((12, 10, 8, 6, 4, 2, 0)) * sign, series((13, 11, 9, 7, 5, 3, 1)) * rest * sign


class Blocks:
    def __init__(self, shape, counts_ref):
        self.n, self.per, self.rows_dev = shape[:3]
        self.ends, self.rest, self.rest_starts, self.rest_places = [], [], [], []
        total, rest_total = 0, 0
        for r in range(self.n):
            count = counts_ref[0, r]
            full = lax.div(count, LANES)
            total = total + full
            self.ends.append(total)
            self.rest.append(count - full * LANES)
            self.rest_starts.append(rest_total)
            self.rest_places.append(r * self.rows_dev + jnp.minimum(full * LANES, self.rows_dev - LANES))
            rest_total = rest_total + self.rest[r]
        self.packed = lax.div(rest_total, LANES)

    def first(self, dest):
        return dest * self.per - jnp.minimum(dest, self.packed)

    def place(self, want):
        slot, begin = 0, 0
        for r in range(self.n - 1):
            past = want >= self.ends[r]
            slot = jnp.where(past, r + 1, slot)
            begin = jnp.where(past, self.ends[r], begin)
        return slot * self.rows_dev + jnp.minimum((want - begin) * LANES, self.rows_dev - LANES)


def over(count, n, step):
    def run(i, _):
        step(i)
        return 0

    lax.fori_loop(0, count, run, 0, unroll=count if n <= 8 else 1)


def pick_kernel(shape, k, size, counts_ref, leg_ref, out_ref, sems):
    blocks = Blocks(shape, counts_ref)
    dest = lax.axis_index("ord") ^ k

    def copy(i, start):
        here = pl.ds(pl.multiple_of(i * LANES, LANES), LANES)
        return pltpu.make_async_copy(leg_ref.at[:, pl.ds(start, LANES)], out_ref.at[:, here], sems.at[i])

    def send(i):
        copy(i, pl.multiple_of(blocks.place(blocks.first(dest) + i), LANES)).start()

    def wait(i):
        copy(i, 0).wait()

    over(size, blocks.n, send)
    over(size, blocks.n, wait)


@functools.partial(jax.jit, static_argnums=(0, 1, 2))
def pick(shape, k, size, counts, legendre):
    rows = legendre.shape[0]
    elements = rows * size * LANES
    return pl.pallas_call(
        functools.partial(pick_kernel, shape, k, size),
        out_shape=jax.ShapeDtypeStruct((rows, size * LANES), jnp.float32),
        in_specs=[pl.BlockSpec(memory_space=SMEM), pl.BlockSpec(memory_space=pltpu.HBM)],
        out_specs=pl.BlockSpec(memory_space=VMEM),
        scratch_shapes=[pltpu.SemaphoreType.DMA((size,))],
        compiler_params=pltpu.CompilerParams(vmem_limit_bytes=56 << 20),
        cost_estimate=pl.CostEstimate(flops=8 * elements, bytes_accessed=8 * elements, transcendentals=0),
        name="pick",
    )(counts, legendre)


def inner_tables(shape, harmonic, tops):
    along = lax.broadcasted_iota(jnp.int32, (SUBS, LANES), 1).astype(jnp.float32) * (track_span / shape[3])
    pairs_of = [wave_pair(harmonic[top : top + SUBS] * along) for top in tops]
    return [(c * shape[4], s * shape[4]) for c, s in pairs_of]


def outer_tables(shape, lon, begin, harmonic, phase, tops):
    longitude = lon + begin.astype(jnp.float32) * (track_span / shape[3])
    return [wave_pair(harmonic[top : top + SUBS] * longitude - phase[top : top + SUBS]) for top in tops]


def wave(outer, inner, i):
    return lane_wide(outer[0], i) * inner[0] - lane_wide(outer[1], i) * inner[1]


def wide_columns(cols_ref):
    rows = cols_ref.shape[0]
    harmonic = jnp.broadcast_to(cols_ref[:, 0:1], (rows, LANES))
    return harmonic, jnp.broadcast_to(cols_ref[:, 1:2] * quarter_turn, (rows, LANES))


def design_kernel(shape, first, size, counts_ref, lon_ref, cols_ref, leg_ref, *refs):
    blocks = Blocks(shape, counts_ref)
    n = blocks.n
    outs, (held, left, table, sems, left_sems) = refs[:n], refs[n:]
    me = lax.axis_index("ord")

    def origin(k):
        return blocks.first(me ^ k) + first

    def copy(spot, start):
        here = pl.ds(pl.multiple_of(spot * LANES, LANES), LANES)
        return pltpu.make_async_copy(leg_ref.at[:, pl.ds(start, LANES)], held.at[:, here], sems.at[spot])

    def copy_rest(r, start):
        here = pl.ds(r * LANES, LANES)
        return pltpu.make_async_copy(leg_ref.at[:, pl.ds(start, LANES)], left.at[:, here], left_sems.at[r])

    def send(i):
        for k in range(n):
            copy(k * size + i, pl.multiple_of(blocks.place(origin(k) + i), LANES)).start()

    over(size, n, send)
    for r in range(n):
        copy_rest(r, pl.multiple_of(blocks.rest_places[r], LANES)).start()
        table[0, r] = blocks.rest[r]
        table[1, r] = blocks.rest_starts[r]
    rows = held.shape[0]
    tops = range(0, rows, SUBS)
    lane = lax.broadcasted_iota(jnp.int32, (SUBS, LANES), 1)
    harmonic, phase = wide_columns(cols_ref)
    inner = inner_tables(shape, harmonic, tops)
    begin = jnp.zeros_like(lane)
    for r in range(n):
        begin = jnp.where(lane == r, blocks.rest_places[r], begin)
    outer = outer_tables(shape, lon_ref[0], begin, harmonic, phase, tops)
    for r in range(n):
        copy_rest(r, 0).wait()
        for t, top in enumerate(tops):
            at = (pl.ds(top, SUBS), pl.ds(r * LANES, LANES))
            left[at] = jnp.where(lane < blocks.rest[r], left[at] * wave(outer[t], inner[t], r), 0.0)
    whole_lane = lax.broadcasted_iota(jnp.int32, (rows, LANES), 1)
    for k in range(n):
        outer = outer_tables(shape, lon_ref[0], blocks.place(origin(k) + lane), harmonic, phase, tops)
        for i in range(size):
            copy(k * size + i, 0).wait()
            for t, top in enumerate(tops):
                tile = held[pl.ds(top, SUBS), pl.ds((k * size + i) * LANES, LANES)]
                outs[k][pl.ds(top, SUBS), pl.ds(i * LANES, LANES)] = tile * wave(outer[t], inner[t], i)

        @pl.when((me ^ k) < blocks.packed)
        def _(k=k):
            here = pl.ds((size - 1) * LANES, LANES)
            outs[k][:, here] = jnp.zeros((rows, LANES), jnp.float32)

            def add(r, _):
                many = table[0, r]
                shift = table[1, r] - (me ^ k) * LANES

                @pl.when((shift < LANES) & (shift + many > 0))
                def _():
                    spot = whole_lane - shift
                    tile = left[:, pl.ds(pl.multiple_of(r * LANES, LANES), LANES)]
                    rolled = pltpu.roll(tile, lax.rem(shift + LANES, LANES), 1)
                    outs[k][:, here] += jnp.where((spot >= 0) & (spot < many), rolled, 0.0)

                return 0

            lax.fori_loop(0, n, add, 0)


@functools.partial(jax.jit, static_argnums=(0, 1, 2))
def design(shape, first, size, counts, lon_center, own, legendre):
    n, rows = shape[0], legendre.shape[0]
    elements = rows * n * size * LANES
    return pl.pallas_call(
        functools.partial(design_kernel, shape, first, size),
        out_shape=[jax.ShapeDtypeStruct((rows, size * LANES), jnp.float32)] * n,
        in_specs=[
            pl.BlockSpec(memory_space=SMEM),
            pl.BlockSpec(memory_space=SMEM),
            pl.BlockSpec(memory_space=VMEM),
            pl.BlockSpec(memory_space=pltpu.HBM),
        ],
        out_specs=[pl.BlockSpec(memory_space=VMEM)] * n,
        scratch_shapes=[
            pltpu.VMEM((rows, n * size * LANES), jnp.float32),
            pltpu.VMEM((rows, n * LANES), jnp.float32),
            pltpu.SMEM((2, n), jnp.int32),
            pltpu.SemaphoreType.DMA((n * size,)),
            pltpu.SemaphoreType.DMA((n,)),
        ],
        compiler_params=pltpu.CompilerParams(vmem_limit_bytes=56 << 20),
        cost_estimate=pl.CostEstimate(flops=8 * elements, bytes_accessed=8 * elements, transcendentals=0),
        name="design",
    )(counts, lon_center, own, legendre)


def lane_wide(x, j):
    return jnp.broadcast_to(x[:, j : j + 1], (SUBS, LANES))


def upper_blocks(cols):
    nb = cols // LANES
    return [(i, j) for i in range(nb) for j in range(i, nb)]


def gram_terms(n, cols, tile, ins, high, low, value, add):
    me = lax.axis_index("ord")
    each, rows = ins[0].shape

    def times(a, b):
        return lax.dot_general(a, b, (((1,), (1,)), ((), ())), preferred_element_type=jnp.float32)

    tall = min(256, cols)
    for s in range(rows // tile):
        for k in range(n):
            begin = pl.multiple_of((me ^ k) * each, each)
            value(s, begin, ins[k], high.at[s % 2], low.at[s % 2])
        for i in range(0, cols, tall):
            hi, lo = high[s % 2, pl.ds(i, tall), :], low[s % 2, pl.ds(i, tall), :]
            his, los = high[s % 2, pl.ds(i, cols - i), :], low[s % 2, pl.ds(i, cols - i), :]
            add(s, (pl.ds(i, tall), pl.ds(i, cols - i)), times(hi, his) + (times(hi, los) + times(lo, his)))


def split(x):
    top = x.astype(jnp.bfloat16)
    return top, (x - top.astype(jnp.float32)).astype(jnp.bfloat16)


def early_kernel(shape, cols, tile, counts_ref, lon_ref, cols_ref, *refs):
    n = shape[0]
    ins, (acc, high, low, inner_ref, outer_ref) = refs[:n], refs[n:]
    blocks = Blocks(shape, counts_ref)
    me = lax.axis_index("ord")
    lane = lax.broadcasted_iota(jnp.int32, (SUBS, LANES), 1)
    begins = blocks.place(blocks.first(me) + lane)
    harmonic, phase = wide_columns(cols_ref)
    tops = range(0, cols, SUBS)
    inner = inner_tables(shape, harmonic, tops)
    outer = outer_tables(shape, lon_ref[0], begins, harmonic, phase, tops)
    for t, top in enumerate(tops):
        for half in range(2):
            inner_ref[half, pl.ds(top, SUBS), :] = inner[t][half]
            outer_ref[half, pl.ds(top, SUBS), :] = outer[t][half]
    each = cols // n
    step = 2 * SUBS

    def value(s, begin, leg, high_ref, low_ref):
        for top in range(0, each, step):
            at = pl.ds(pl.multiple_of(begin + top, step), step)
            inside = [inner_ref[half, at, :] for half in range(2)]
            outside = [outer_ref[half, at, :] for half in range(2)]
            for i in range(tile // LANES):
                b = s * (tile // LANES) + i
                c, d = (jnp.broadcast_to(x[:, b : b + 1], (step, LANES)) for x in outside)
                x = leg[pl.ds(top, step), pl.ds(b * LANES, LANES)] * (c * inside[0] - d * inside[1])
                here = (at, pl.ds(i * LANES, LANES))
                high_ref[here], low_ref[here] = split(x)

    def add(s, at, block):
        acc[at] = acc[at] + block if s else block

    gram_terms(n, cols, tile, ins, high, low, value, add)


def late_kernel(n, cols, tile, *refs):
    ins, (before, keep, give, high, low, acc, packed) = refs[:n], refs[n:]
    me = lax.axis_index("ord")
    each = cols // n

    def value(s, begin, part, high_ref, low_ref):
        at = pl.ds(begin, each)
        high_ref[at, :], low_ref[at, :] = split(part[:, pl.ds(s * tile, tile)])

    def add(s, at, block):
        acc[at] = (acc[at] if s else before[at]) + block

    gram_terms(n, cols, tile, ins, high, low, value, add)
    for t, (i, j) in enumerate(upper_blocks(cols)):
        packed[pl.ds(t * LANES, LANES), :] = acc[pl.ds(i * LANES, LANES), pl.ds(j * LANES, LANES)]
    piece = packed.shape[0] // n
    for k in range(n):
        there = packed[pl.ds(pl.multiple_of((me ^ k) * piece, SUBS), piece), :]
        (give if k % 2 else keep)[pl.ds(k // 2 * piece, piece), :] = there


def tile_of(rows):
    return max(t for t in range(LANES, 641, LANES) if rows % t == 0)


def early_gram(shape, counts, lon_center, columns, parts):
    n = shape[0]
    each, rows = parts[0].shape
    cols, tile = each * n, tile_of(rows)
    vmem = pl.BlockSpec(memory_space=VMEM)
    return pl.pallas_call(
        functools.partial(early_kernel, shape, cols, tile),
        out_shape=jax.ShapeDtypeStruct((cols, cols), jnp.float32),
        in_specs=[pl.BlockSpec(memory_space=SMEM)] * 2 + [vmem] * (n + 1),
        out_specs=vmem,
        scratch_shapes=[pltpu.VMEM((2, cols, tile), jnp.bfloat16)] * 2
        + [pltpu.VMEM((2, cols, LANES), jnp.float32)] * 2,
        compiler_params=pltpu.CompilerParams(vmem_limit_bytes=32 << 20),
        cost_estimate=pl.CostEstimate(flops=0, bytes_accessed=0, transcendentals=0),
        name="gram",
    )(counts, lon_center, columns, *parts)


def late_gram(n, parts, before):
    each, rows = parts[0].shape
    cols, tile = each * n, tile_of(rows)
    height = len(upper_blocks(cols)) * LANES
    vmem = pl.BlockSpec(memory_space=VMEM)
    return pl.pallas_call(
        functools.partial(late_kernel, n, cols, tile),
        out_shape=[jax.ShapeDtypeStruct((height // 2, LANES), jnp.float32)] * 2,
        in_specs=[vmem] * (n + 1),
        out_specs=[vmem] * 2,
        scratch_shapes=[pltpu.VMEM((2, cols, tile), jnp.bfloat16)] * 2
        + [pltpu.VMEM((cols, cols), jnp.float32), pltpu.VMEM((height, LANES), jnp.float32)],
        compiler_params=pltpu.CompilerParams(vmem_limit_bytes=32 << 20),
        cost_estimate=pl.CostEstimate(
            flops=6 * cols * cols * rows, bytes_accessed=4 * cols * rows, transcendentals=0
        ),
        name="gram_late",
    )(*parts, before)


def row_wide(ref, row, column):
    return jnp.broadcast_to(ref[pl.ds(row, 1), pl.ds(column, LANES)], (SUBS, LANES))


def factor_panel(a_ref, r_ref, u_ref, t_ref, base, p, wide, lane, sub, columns):
    groups = LANES // SUBS
    row0, c0 = base + SUBS * p, SUBS * p
    slot = (p % 2) * SUBS * SUBS
    if columns is None:
        own = a_ref[pl.ds(row0, SUBS), pl.ds(base, LANES)]
        columns = [lane_wide(own, c0 + j) for j in range(SUBS)]
    for j in range(SUBS):
        u_ref[pl.ds(slot + SUBS * j, SUBS), :] = columns[j]
    d = {(i, j): row_wide(u_ref, slot + SUBS * j + i, 0) for j in range(SUBS) for i in range(j + 1)}
    inv, up = [None] * SUBS, {}
    for i in range(SUBS):
        inv[i] = lax.rsqrt(d[i, i])
        for j in range(i + 1, SUBS):
            up[i, j] = d[i, j] * inv[i]
        for a in range(i + 1, SUBS):
            for b in range(a, SUBS):
                d[a, b] = d[a, b] - up[i, a] * up[i, b]
    coef, following = [], None
    if p + 1 < groups:
        below = a_ref[pl.ds(row0 + SUBS, SUBS), pl.ds(base, LANES)]
        for j in range(SUBS):
            acc = lane_wide(below, c0 + j)
            for i in range(j):
                acc = acc - up[i, j] * coef[i]
            coef.append(acc * inv[j])
            t_ref[pl.ds(slot + SUBS * j, SUBS), :] = coef[j]
        following = [
            lane_wide(below, c0 + SUBS + b)
            - tree_sum([coef[j] * row_wide(t_ref, slot + SUBS * j + b, 0) for j in range(SUBS)])
            for b in range(SUBS)
        ]
    done = [[None] * SUBS for _ in range(wide)]
    for w in range(wide):
        for i in range(SUBS):
            acc = row_wide(a_ref, row0 + i, base + LANES * w)
            for j in range(i):
                acc = acc - up[j, i] * done[w][j]
            done[w][i] = acc * inv[i]

    def update(g, coef, rows):
        for w in range(wide):
            at = (pl.ds(base + SUBS * g, SUBS), pl.ds(base + LANES * w, LANES))
            a_ref[at] = a_ref[at] - tree_sum([coef[j] * rows[w][j] for j in range(SUBS)])

    if p + 1 < groups:
        update(p + 1, coef, done)
    if p + 2 < groups:
        solved = [[None] * SUBS for _ in range(wide)]
        for w in range(wide):
            for i in range(SUBS - 1, -1, -1):
                acc = done[w][i]
                for j in range(i + 1, SUBS):
                    acc = acc - up[i, j] * solved[w][j]
                solved[w][i] = acc * inv[i]
        for g in range(p + 2, groups):
            below = a_ref[pl.ds(base + SUBS * g, SUBS), pl.ds(base, LANES)]
            update(g, [lane_wide(below, c0 + j) for j in range(SUBS)], solved)
    for w in range(wide):
        out = done[w][0]
        for i in range(1, SUBS):
            out = jnp.where(sub == i, done[w][i], out)
        if w == 0:
            out = jnp.where(lane >= sub + c0, out, 0.0)
        r_ref[pl.ds(row0, SUBS), pl.ds(base + LANES * w, LANES)] = out
    return following


def factor_kernel(n, cols, kaula_ref, *refs):
    ins, (r_ref, a_ref, packed, u_ref, t_ref) = refs[:n], refs[n:]
    me = lax.axis_index("ord")
    piece = packed.shape[0] // n
    for k in range(n):
        packed[pl.ds(pl.multiple_of((me ^ k) * piece, SUBS), piece), :] = ins[k][...]
    square = (LANES, LANES)
    diag = lax.broadcasted_iota(jnp.int32, square, 0) == lax.broadcasted_iota(jnp.int32, square, 1)
    for t, (i, j) in enumerate(upper_blocks(cols)):
        block = packed[pl.ds(t * LANES, LANES), :]
        if i == j:
            block = block + jnp.where(diag, kaula_ref[:, pl.ds(i * LANES, LANES)], 0.0)
        a_ref[pl.ds(i * LANES, LANES), pl.ds(j * LANES, LANES)] = block
    lane = lax.broadcasted_iota(jnp.int32, (SUBS, LANES), 1)
    sub = lax.broadcasted_iota(jnp.int32, (SUBS, LANES), 0)
    count = cols // LANES
    for k in range(count):
        base, wide = k * LANES, count - k
        if base:
            r_ref[pl.ds(base, LANES), pl.ds(0, base)] = jnp.zeros((LANES, base), jnp.float32)
        columns = None
        for p in range(LANES // SUBS):
            columns = factor_panel(a_ref, r_ref, u_ref, t_ref, base, p, wide, lane, sub, columns)
        for i in range(k + 1, count):
            left = r_ref[pl.ds(base, LANES), pl.ds(i * LANES, LANES)]
            right = r_ref[pl.ds(base, LANES), pl.ds(i * LANES, cols - i * LANES)]
            a_ref[pl.ds(i * LANES, LANES), pl.ds(i * LANES, cols - i * LANES)] -= lax.dot_general(
                left,
                right,
                (((0,), (0,)), ((), ())),
                precision=lax.Precision.HIGHEST,
                preferred_element_type=jnp.float32,
            )


def factor(n, cols, kaula_square, pieces):
    height = len(upper_blocks(cols)) * LANES
    return pl.pallas_call(
        functools.partial(factor_kernel, n, cols),
        out_shape=jax.ShapeDtypeStruct((cols, cols), jnp.float32),
        in_specs=[pl.BlockSpec(memory_space=VMEM)] * (n + 1),
        out_specs=pl.BlockSpec(memory_space=VMEM),
        scratch_shapes=[
            pltpu.VMEM((cols, cols), jnp.float32),
            pltpu.VMEM((height, LANES), jnp.float32),
            pltpu.VMEM((2 * SUBS * SUBS, LANES), jnp.float32),
            pltpu.VMEM((2 * SUBS * SUBS, LANES), jnp.float32),
        ],
        compiler_params=pltpu.CompilerParams(vmem_limit_bytes=32 << 20),
        name="factor",
    )(kaula_square, *pieces)


def pairs(size, k):
    return [(i, i ^ k) for i in range(size)]


def swap(x, axis, k):
    return lax.ppermute(x, axis, pairs(lax.axis_size(axis), k)) if k else x


def tree_sum(terms):
    while len(terms) > 1:
        terms = [a + b for a, b in zip(terms[::2], terms[1::2])]
    return terms[0]


def body(legendre, lon_center, counts, column_index):
    n, groups = lax.axis_size("ord"), lax.axis_size("grp")
    cols_dev, rows_grp = legendre.shape
    cols = cols_dev * n
    rows_dev = rows_grp // n
    valid_rows = 3 * rows_grp // 4
    per = valid_rows // LANES // n
    late = max(1, per // 6)
    early = per - late
    shape = (n, per, rows_dev, rows_grp, 1.0 / math.sqrt(rows_grp * groups))
    columns = column_index[1:3].astype(jnp.float32).T
    own = lax.dynamic_slice_in_dim(columns, lax.axis_index("ord") * cols_dev, cols_dev, 0)
    far = sorted(range(1, n), key=lambda k: (-bin(k >> 1).count("1"), k))
    early_parts = [None] * n
    for k in far:
        early_parts[k] = swap(pick(shape, k, early, counts, legendre), "ord", k)
    gate = far[1]
    early_parts[gate], now = lax.optimization_barrier((early_parts[gate], counts))
    early_parts[0], now = lax.optimization_barrier((pick(shape, 0, early, now, legendre), now))
    late_parts = design(shape, early, late, now, lon_center, own, legendre)
    late_parts = [swap(late_parts[k], "ord", k) for k in range(n)]
    before = early_gram(shape, counts, lon_center, columns, early_parts)
    keep, give = late_gram(n, late_parts, before)
    half = (keep + swap(give, "ord", 1)).reshape(n // 2, -1, LANES)
    share = tree_sum([swap(half[c], "ord", 2 * c) for c in range(n // 2)])
    share = tree_sum([swap(share, "grp", k) for k in range(groups)])
    gathered = []
    for c in range(n // 2):
        there = swap(share, "ord", 2 * c)
        gathered += [there, swap(there, "ord", 1)]
    degree = column_index[0:1].astype(jnp.float32)
    kaula_weight = kaula_gain * (degree / NMAX) ** 2
    return factor(n, cols, kaula_weight * kaula_weight, gathered)


def solution(mesh):
    placed = (P("ord", "grp"), P("grp"), P("grp", None), P())
    return jax.shard_map(body, mesh=mesh, in_specs=placed, out_specs=P(), check_vma=False)
```
